32 devices in a mesh: cfg: 2 (over x), uly: 4 (over y, core), blk: 4 (over z).
Axes of the slice: x: 2, y: 2, z: 4, core: 2. Of those that a mesh axis runs over, the one named last changes fastest.
Arguments:
- queries: bfloat16 [4096, 2048], P(('cfg', 'uly', 'blk')), parts along dimension 0, may hold values from -120 to 120
- keys: bfloat16 [4096, 2048], P(('cfg', 'uly', 'blk')), parts along dimension 0, may hold values from -10 to 10
- values: bfloat16 [4096, 2048], P(('cfg', 'uly', 'blk')), parts along dimension 0, may hold values from -6 to 6
- text_keys: bfloat16 [512, 2048], P('cfg'), parts along dimension 0, may hold values from -9 to 9
- text_values: bfloat16 [512, 2048], P('cfg'), parts along dimension 0, may hold values from -6 to 6
- text_len: int32 [2], P('cfg'), parts along dimension 0, may hold values from 1 to 256
- residual: bfloat16 [4096, 3072], P(('cfg', 'uly', 'blk')), parts along dimension 0, may hold values from -4 to 4
- mlp_term: bfloat16 [4096, 3072], P(('cfg', 'uly', 'blk')), parts along dimension 0, may hold values from -4 to 4
- gate: float32 [3072], replicated, may hold values from 0.5 to 2
- final_shift: float32 [3072], replicated, may hold values from -3 to 3
- final_scale: float32 [3072], replicated, may hold values from -0.5 to 0.5
- final_weight: bfloat16 [3072, 64], replicated, may hold values from -0.109375 to 0.109375
- final_bias: float32 [64], replicated, may hold values from -3 to 3
- out_weight: bfloat16 [2048, 3072], replicated, may hold values from -0.125 to 0.125
- uncond_velocity: float32 [4096, 64], P(('cfg', 'uly', 'blk')), parts along dimension 0, may hold values from -6 to 6
- latents: float32 [4096, 64], P(('cfg', 'uly', 'blk')), parts along dimension 0, may hold values from -6 to 6
- timestep: int32 [1], replicated, may hold values from 0 to 49
- guidance: int32 [1], replicated, may hold values from 15 to 90
Outputs:
- velocity: float32 [4096, 64], P(('cfg', 'uly', 'blk')), parts along dimension 0
- next_latents: float32 [4096, 64], P(('cfg', 'uly', 'blk')), parts along dimension 0
The draws below stay inside these ranges and needn't reach their ends.
There are 2 independent parts, one for each index of `cfg`. The reference program is written for one: setup_inputs(seed, part) draws one part's arguments, and reference() takes and returns one part's arrays. A program takes and returns all parts, laid end to end along the dimension named above; an argument that names none is the same for every part. Nothing has to cross between parts.
All inputs are finite; a program needn't handle non-finite values.
Results may differ from the reference program's by a relative error of at most 0.0065.
Values may be sent and summed in bfloat16 or wider, within the bound.
A program may use at most 128 MiB of HBM per device.

```python
import math
import jax
import jax.numpy as jnp
from jax import lax

D = 3072
HEADS = 16
HD = 128
TXT = 256
CH = 64
STEPS = 50
IMG = 2048


def common_normals(key):
    return jnp.clip(jax.random.normal(key, (IMG, HEADS * HD), jnp.float32), -6.0, 6.0)


def draw_keys(key, part):
    shared = common_normals(key)
    result = 1.5 * shared
    return result.astype(jnp.bfloat16)


def draw_queries(key, part):
    key = jax.random.fold_in(key, 7)
    result = 1.5 * jnp.clip(jax.random.normal(key, (IMG, HEADS * HD), jnp.float32), -6.0, 6.0)
    return result.astype(jnp.bfloat16)


def steps_of(key, shape, split, smallest, top_value):
    level = 1.0
    for dim, parts in split:
        draws = jax.random.uniform(jax.random.fold_in(jax.random.fold_in(key, 6), dim), (parts,), jnp.float32, smallest / len(split), top_value / len(split))
        level = level * jnp.repeat(jnp.exp(draws), shape[dim] // parts).reshape((-1,) + (1,) * (len(shape) - 1 - dim))
    return level


def bell_draw(rng, extent, deviation, most, pieces=(), dtype=jnp.bfloat16):
    loudness = steps_of(rng, extent, pieces, -0.22, 0.18) if pieces else 1.0
    values = jax.random.normal(rng, extent, jnp.float32) * deviation * loudness
    return jnp.minimum(jnp.maximum(values, -most), most).astype(dtype)


def setup_inputs(seed: int = 0, part: int = 0) -> dict:
    seeds = jax.random.split(jax.random.key(seed), 19)
    own_keys = jax.random.split(jax.random.fold_in(seeds[18], part), 19)
    queries = draw_queries(jax.random.fold_in(jax.random.fold_in(seeds[18], part), 71), part)
    keys = draw_keys(jax.random.fold_in(jax.random.fold_in(seeds[18], part), 71), part)
    values = bell_draw(own_keys[2], (IMG, HEADS * HD), 1.0, 6.0, ((0, 16),))
    text_keys = bell_draw(own_keys[3], (TXT, HEADS * HD), 1.5, 9.0)
    text_values = bell_draw(own_keys[4], (TXT, HEADS * HD), 1.0, 6.0)
    text_len = jax.random.randint(own_keys[5], (1,), 1, TXT + 1).astype(jnp.int32)
    residual = bell_draw(own_keys[6], (IMG, D), 0.3, 4.0, ((0, 16),))
    mlp_term = bell_draw(own_keys[7], (IMG, D), 0.3, 4.0, ((0, 16),))
    gate = jnp.clip(jax.random.uniform(seeds[8], (D,), jnp.float32, 0.5, 2.0), 0.5, 2.0)
    final_shift = bell_draw(seeds[9], (D,), 0.5, 3.0, (), jnp.float32)
    final_scale = jnp.clip(jax.random.uniform(seeds[10], (D,), jnp.float32, -0.5, 0.5), -0.5, 0.5)
    final_weight = bell_draw(seeds[11], (D, CH), D ** -0.5, 0.109375)
    final_bias = bell_draw(seeds[12], (CH,), 0.5, 3.0, (), jnp.float32)
    out_weight = bell_draw(seeds[13], (HEADS * HD, D), (HEADS * HD) ** -0.5, 0.125)
    uncond_velocity = bell_draw(own_keys[14], (IMG, CH), 1.0, 6.0, ((0, 16),), jnp.float32)
    latents = bell_draw(own_keys[15], (IMG, CH), 1.0, 6.0, ((0, 16),), jnp.float32)
    timestep = jax.random.randint(seeds[16], (1,), 0, STEPS).astype(jnp.int32)
    guidance = jax.random.randint(seeds[17], (1,), 15, 91).astype(jnp.int32)
    return dict(queries=queries, keys=keys, values=values, text_keys=text_keys, text_values=text_values, text_len=text_len, residual=residual, mlp_term=mlp_term, gate=gate, final_shift=final_shift, final_scale=final_scale, final_weight=final_weight, final_bias=final_bias, out_weight=out_weight, uncond_velocity=uncond_velocity, latents=latents, timestep=timestep, guidance=guidance)


def power_of_two(exponent):
    shifted = exponent + 64
    result = jnp.full(exponent.shape, 2.0 ** (-64), jnp.float32)
    for position in range(7):
        result = jnp.where(shifted // 2 ** position % 2 == 1, result * 2.0 ** 2 ** position, result)
    return result

def floor_log2(magnitude, lowest, highest):
    octave = jnp.full(magnitude.shape, lowest, jnp.int32)
    for degree in range(lowest + 1, highest + 1):
        octave = octave + (magnitude >= 2.0 ** degree).astype(jnp.int32)
    return octave

def coarse_grid(scaled):
    magnitude = jnp.abs(scaled)
    octave = floor_log2(magnitude, -6, 8)
    ratio = magnitude * power_of_two(3 - octave)
    nearest = jnp.floor(ratio + 0.5)
    halfway = nearest - ratio == 0.5
    is_odd = nearest - 2.0 * jnp.floor(nearest * 0.5) == 1.0
    nearest = jnp.where(halfway & is_odd, nearest - 1.0, nearest)
    return jnp.sign(scaled) * jnp.minimum(nearest * power_of_two(octave - 3), 448.0)

def block_round(entries):
    count = entries.shape[0]
    width = entries.shape[1]
    blocks = entries.astype(jnp.float32).reshape(count, width // 32, 32)
    largest = lax.optimization_barrier(jnp.max(jnp.abs(blocks), axis=2))
    exponent = floor_log2(largest, -20, 7) - 8
    payload = coarse_grid(blocks * power_of_two(-exponent)[:, :, None]).astype(jnp.bfloat16)
    decoded = payload.astype(jnp.float32) * power_of_two(exponent)[:, :, None]
    return decoded.reshape(count, width).astype(jnp.bfloat16)

def sigma_of(moment):
    return 7.0 * moment / (1.0 + 6.0 * moment)

def reference(queries, keys, values, text_keys, text_values, text_len, residual, mlp_term, gate, final_shift, final_scale, final_weight, final_bias, out_weight, uncond_velocity, latents, timestep, guidance):
    scaling = 1.0 / math.sqrt(HD)
    query_all = block_round(queries).reshape(IMG, HEADS, HD).transpose(1, 0, 2)
    key_all = jnp.concatenate([block_round(keys), text_keys], axis=0).reshape(IMG + TXT, HEADS, HD).transpose(1, 0, 2)
    value_all = jnp.concatenate([block_round(values), text_values], axis=0).reshape(IMG + TXT, HEADS, HD).transpose(1, 0, 2)
    valid = jnp.arange(IMG + TXT) < IMG + text_len[0]
    block_rows = 512 if IMG % 512 == 0 else IMG

    def per_head(inputs):
        head_q, head_k, head_v = inputs

        def per_block(rows):
            scores = jnp.dot(rows, head_k.T, preferred_element_type=jnp.float32) * scaling
            scores = jnp.where(valid[None, :], scores, -jnp.inf)
            peak = lax.optimization_barrier(jnp.max(scores, axis=1, keepdims=True))
            weights = jnp.exp(scores - peak)
            total = lax.optimization_barrier(jnp.sum(weights, axis=1, keepdims=True))
            mixed = jnp.dot(weights.astype(jnp.bfloat16), head_v, preferred_element_type=jnp.float32) / total
            return mixed.astype(jnp.bfloat16)
        blocks = lax.map(per_block, head_q.reshape(IMG // block_rows, block_rows, HD))
        return blocks.reshape(IMG, HD)
    attention = lax.map(per_head, (query_all, key_all, value_all))
    attention = attention.transpose(1, 0, 2).reshape(IMG, HEADS * HD)
    projected = jnp.dot(attention, out_weight, preferred_element_type=jnp.float32)
    hidden = residual.astype(jnp.float32) + gate[None, :] * (projected + mlp_term.astype(jnp.float32))
    center = lax.optimization_barrier(jnp.mean(hidden, axis=1, keepdims=True))
    spread = lax.optimization_barrier(jnp.mean((hidden - center) ** 2, axis=1, keepdims=True))
    normed = (hidden - center) / jnp.sqrt(spread + 1e-06)
    modulated = (normed * (1.0 + final_scale[None, :]) + final_shift[None, :]).astype(jnp.bfloat16)
    cond_velocity = jnp.dot(modulated, final_weight, preferred_element_type=jnp.float32) + final_bias[None, :]
    factor = guidance[0].astype(jnp.float32) / 10.0
    velocity = uncond_velocity + factor * (cond_velocity - uncond_velocity)
    index = timestep[0].astype(jnp.float32)
    delta = sigma_of(1.0 - (index + 1.0) / STEPS) - sigma_of(1.0 - index / STEPS)
    next_latents = latents + delta * velocity
    return (velocity, next_latents)
```

```python
import functools
import math

import jax
import jax.numpy as jnp
from jax import lax
from jax.experimental import pallas as pl
from jax.experimental.pallas import tpu as pltpu
from jax.sharding import PartitionSpec as P

HEADS = 16
HD = 128
STEPS = 50


def power_of_two(exponent):
    shifted = exponent + 64
    result = jnp.full(exponent.shape, 2.0 ** (-64), jnp.float32)
    for position in range(7):
        result = jnp.where(shifted // 2**position % 2 == 1, result * 2.0**2**position, result)
    return result


def floor_log2(magnitude, lowest, highest):
    octave = jnp.full(magnitude.shape, lowest, jnp.int32)
    for degree in range(lowest + 1, highest + 1):
        octave = octave + (magnitude >= 2.0**degree).astype(jnp.int32)
    return octave


def coarse_grid(scaled):
    magnitude = jnp.abs(scaled)
    octave = floor_log2(magnitude, -6, 8)
    ratio = magnitude * power_of_two(3 - octave)
    nearest = jnp.floor(ratio + 0.5)
    halfway = nearest - ratio == 0.5
    is_odd = nearest - 2.0 * jnp.floor(nearest * 0.5) == 1.0
    nearest = jnp.where(halfway & is_odd, nearest - 1.0, nearest)
    return jnp.sign(scaled) * jnp.minimum(nearest * power_of_two(octave - 3), 448.0)


def encode_blocks(entries):
    count, heads_here, width = entries.shape
    blocks = entries.astype(jnp.float32).reshape(count, heads_here, width // 32, 32)
    largest = jnp.max(jnp.abs(blocks), axis=3)
    exponent = floor_log2(largest, -20, 7) - 8
    payload = coarse_grid(blocks * power_of_two(-exponent)[:, :, :, None])
    return (payload.reshape(count, heads_here, width).astype(jnp.bfloat16), exponent)


def decode_blocks(payload, exponent):
    count, heads_here, width = payload.shape
    blocks = payload.astype(jnp.float32).reshape(count, heads_here, width // 32, 32)
    decoded = blocks * power_of_two(exponent)[:, :, :, None]
    return decoded.reshape(count, heads_here, width).astype(jnp.bfloat16)


def text_start(query_rows, text_key_heads, text_value_heads, text_len):
    scaling = 1.0 / math.sqrt(HD)
    scores = (
        jnp.einsum("shd,thd->sht", query_rows, text_key_heads, preferred_element_type=jnp.float32)
        * scaling
    )
    valid = jnp.arange(text_key_heads.shape[0]) < text_len[0]
    scores = jnp.where(valid[None, None, :], scores, -jnp.inf)
    peak = jnp.max(scores, axis=2)
    weights = jnp.exp(scores - peak[:, :, None])
    total = jnp.sum(weights, axis=2)
    summed = jnp.einsum(
        "sht,thd->shd",
        weights.astype(jnp.bfloat16),
        text_value_heads,
        preferred_element_type=jnp.float32,
    )
    return (peak, total, summed)


def attend_block(running, query_rows, block_keys, block_values):
    scaling = 1.0 / math.sqrt(HD)
    peak, total, summed = running
    scores = (
        jnp.einsum("shd,khd->shk", query_rows, block_keys, preferred_element_type=jnp.float32)
        * scaling
    )
    new_peak = jnp.maximum(peak, jnp.max(scores, axis=2))
    correction = jnp.exp(peak - new_peak)
    weights = jnp.exp(scores - new_peak[:, :, None])
    total = total * correction + jnp.sum(weights, axis=2)
    added = jnp.einsum(
        "shk,khd->shd",
        weights.astype(jnp.bfloat16),
        block_values,
        preferred_element_type=jnp.float32,
    )
    summed = summed * correction[:, :, None] + added
    return (new_peak, total, summed)


def key_fold(carried, portion, query_rows):
    key_part, value_part = portion
    count = key_part.shape[0]
    width = 512
    key_blocks = key_part.reshape((count // width, width) + key_part.shape[1:])
    value_blocks = value_part.reshape((count // width, width) + value_part.shape[1:])

    def one_block(running, blocks):
        return (attend_block(running, query_rows, blocks[0], blocks[1]), None)

    final_state, unused = lax.scan(one_block, carried, (key_blocks, value_blocks))
    return final_state


def finish_rows(carried):
    peak, total, summed = carried
    return (summed / total[:, :, None]).astype(jnp.bfloat16)


def sigma_of(moment):
    return 7.0 * moment / (1.0 + 6.0 * moment)


def body(
    queries,
    keys,
    values,
    text_keys,
    text_values,
    text_len,
    residual,
    mlp_term,
    gate,
    final_shift,
    final_scale,
    final_weight,
    final_bias,
    out_weight,
    uncond_velocity,
    latents,
    timestep,
    guidance,
):
    rows_here = queries.shape[0]
    query_three = queries.reshape(rows_here, HEADS, HD)
    key_three = keys.reshape(rows_here, HEADS, HD)
    value_three = values.reshape(rows_here, HEADS, HD)
    text_key_three = text_keys.reshape(text_keys.shape[0], HEADS, HD)
    text_value_three = text_values.reshape(text_values.shape[0], HEADS, HD)
    query_pay, query_exp = encode_blocks(query_three)
    key_pay, key_exp = encode_blocks(key_three)
    value_pay, value_exp = encode_blocks(value_three)
    local_heads = HEADS // lax.axis_size("uly")
    first_head = lax.axis_index("uly") * local_heads
    query_pay, query_exp, key_pay, key_exp, value_pay, value_exp = (
        lax.all_to_all(query_pay, "uly", split_axis=1, concat_axis=0, tiled=True),
        lax.all_to_all(query_exp, "uly", split_axis=1, concat_axis=0, tiled=True),
        lax.all_to_all(key_pay, "uly", split_axis=1, concat_axis=0, tiled=True),
        lax.all_to_all(key_exp, "uly", split_axis=1, concat_axis=0, tiled=True),
        lax.all_to_all(value_pay, "uly", split_axis=1, concat_axis=0, tiled=True),
        lax.all_to_all(value_exp, "uly", split_axis=1, concat_axis=0, tiled=True),
    )
    query_rows = decode_blocks(query_pay, query_exp)
    key_rows = decode_blocks(key_pay, key_exp)
    value_rows = decode_blocks(value_pay, value_exp)
    text_key_heads = lax.dynamic_slice_in_dim(text_key_three, first_head, local_heads, 1)
    text_value_heads = lax.dynamic_slice_in_dim(text_value_three, first_head, local_heads, 1)
    initial = text_start(query_rows, text_key_heads, text_value_heads, text_len)
    carried = key_fold(
        initial,
        (
            lax.all_gather(key_rows, "blk", axis=0, tiled=True),
            lax.all_gather(value_rows, "blk", axis=0, tiled=True),
        ),
        query_rows,
    )
    attention_rows = lax.all_to_all(
        finish_rows(carried), "uly", split_axis=0, concat_axis=1, tiled=True
    )
    attention = attention_rows.reshape(rows_here, HEADS * HD)
    projected = jnp.dot(attention, out_weight, preferred_element_type=jnp.float32)
    hidden = residual.astype(jnp.float32) + gate[None, :] * (
        projected + mlp_term.astype(jnp.float32)
    )
    center = jnp.mean(hidden, axis=1, keepdims=True)
    spread = jnp.mean((hidden - center) ** 2, axis=1, keepdims=True)
    normed = (hidden - center) / jnp.sqrt(spread + 1e-06)
    modulated = (normed * (1.0 + final_scale[None, :]) + final_shift[None, :]).astype(jnp.bfloat16)
    cond_velocity = (
        jnp.dot(modulated, final_weight, preferred_element_type=jnp.float32) + final_bias[None, :]
    )
    factor = guidance[0].astype(jnp.float32) / 10.0
    velocity = uncond_velocity + factor * (cond_velocity - uncond_velocity)
    index = timestep[0].astype(jnp.float32)
    delta = sigma_of(1.0 - (index + 1.0) / STEPS) - sigma_of(1.0 - index / STEPS)
    next_latents = latents + delta * velocity
    return (velocity, next_latents)


CHUNK = 2


def block_round(entries, spread_matrix):
    x = entries.astype(jnp.float32)
    size = jnp.abs(x)
    top = size
    for shift in (1, 2, 4, 8, 16):
        top = jnp.maximum(top, pltpu.roll(top, shift, 1))
    top = jnp.maximum(top, 2.0**-20)
    top = top * 0.7515
    carrier = top * 2.0**23
    top = (top + carrier) - carrier
    scale = jnp.dot(
        top.astype(jnp.bfloat16), spread_matrix, preferred_element_type=jnp.float32
    )
    carrier = jnp.maximum(size * 2.0**20, scale * 96.0)
    rounded = (x + carrier) - carrier
    limit = scale * 1.75
    return jnp.minimum(jnp.maximum(rounded, -limit), limit).astype(jnp.bfloat16)


def fused_kernel(
    uly_size,
    blk_size,
    q_hbm,
    k_hbm,
    v_hbm,
    tk_hbm,
    tv_hbm,
    text_len,
    res_hbm,
    mlp_hbm,
    gate,
    shift,
    scale,
    fw_hbm,
    bias,
    ow_hbm,
    uncond,
    latents,
    timestep,
    guidance,
    vel_out,
    next_out,
    raw,
    coded,
    qbuf,
    kbuf,
    vbuf,
    obuf,
    att,
    weight,
    res,
    mlp,
    fw,
    load_sem,
    weight_sem,
    send_sem,
    recv_sem,
    osend_sem,
    orecv_sem,
):
    n = uly_size * blk_size
    rows = raw.shape[1]
    uly = lax.axis_index("uly")
    blk = lax.axis_index("blk")
    me = uly * blk_size + blk

    def ahead(j):
        return lax.rem(uly + lax.rem(j, uly_size), uly_size), lax.rem(
            blk + j // uly_size, blk_size
        )

    def behind(j):
        return lax.rem(uly + uly_size - lax.rem(j, uly_size), uly_size), lax.rem(
            blk + blk_size - j // uly_size, blk_size
        )

    barrier = pltpu.get_barrier_semaphore()

    def greet(j, unused):
        u, b = ahead(j)
        pl.semaphore_signal(
            barrier, inc=1, device_id={"uly": u, "blk": b}, device_id_type=pl.DeviceIdType.MESH
        )
        return unused

    own = pl.ds(pl.multiple_of(me * HD, HD), HD)
    text = tk_hbm.shape[0]
    loads = [
        pltpu.make_async_copy(k_hbm, raw.at[0], load_sem.at[0]),
        pltpu.make_async_copy(v_hbm, raw.at[1], load_sem.at[1]),
        pltpu.make_async_copy(q_hbm, raw.at[2], load_sem.at[2]),
        pltpu.make_async_copy(tk_hbm.at[:, own], kbuf.at[pl.ds(n * rows, text)], load_sem.at[3]),
        pltpu.make_async_copy(tv_hbm.at[:, own], vbuf.at[pl.ds(n * rows, text)], load_sem.at[4]),
        pltpu.make_async_copy(res_hbm, res, load_sem.at[5]),
        pltpu.make_async_copy(mlp_hbm, mlp, load_sem.at[6]),
        pltpu.make_async_copy(fw_hbm, fw, load_sem.at[7]),
    ]
    for load in loads:
        load.start()
    lax.fori_loop(1, n, greet, 0)

    lane_from = lax.broadcasted_iota(jnp.int32, (HD, HD), 0)
    lane_to = lax.broadcasted_iota(jnp.int32, (HD, HD), 1)
    spread_matrix = jnp.where(lane_from == lane_to // 32 * 32 + 31, 1.0, 0.0).astype(jnp.bfloat16)

    def slot(j):
        return pl.ds(pl.multiple_of(j * rows, rows), rows)

    def outgoing(kind, target, j):
        u, b = ahead(j)
        return pltpu.make_async_remote_copy(
            src_ref=coded.at[kind, slot(j)],
            dst_ref=target.at[slot(j)],
            send_sem=send_sem.at[kind, j],
            recv_sem=recv_sem.at[kind, j],
            device_id={"uly": u, "blk": b},
            device_id_type=pl.DeviceIdType.MESH,
        )

    def weight_load(j):
        u, b = ahead(j)
        start = pl.multiple_of((u * blk_size + b) * HD, HD)
        return pltpu.make_async_copy(
            ow_hbm.at[pl.ds(start, HD)], weight.at[slot(j) if rows == HD else pl.ds(j * HD, HD)],
            weight_sem.at[j],
        )

    for kind, target in ((0, kbuf), (1, vbuf), (2, qbuf)):
        loads[kind].wait()

        def code(j):
            u, b = ahead(j)
            columns = pl.ds(pl.multiple_of((u * blk_size + b) * HD, HD), HD)
            return block_round(raw[kind, :, columns], spread_matrix)

        if kind == 0:

            def code_only(i, unused):
                j = n - 1 - i
                coded[kind, slot(j), :] = code(j)
                return unused

            lax.fori_loop(0, 2, code_only, 0)
            pl.semaphore_wait(barrier, n - 1)
            outgoing(kind, target, n - 1).start()
            outgoing(kind, target, n - 2).start()
            first = 2
        else:
            first = 0

        def code_and_send(i, unused):
            j = n - 1 - i
            coded[kind, slot(j), :] = code(j)
            outgoing(kind, target, j).start()
            return unused

        lax.fori_loop(first, n - 1, code_and_send, 0)
        target[pl.ds(0, rows), :] = code(0)

    def start_weight(i, unused):
        weight_load(n - 1 - i).start()
        return unused

    lax.fori_loop(0, n, start_weight, 0)

    def wait_recv(kind, target):
        def one(i, unused):
            outgoing(kind, target, n - 1 - i).wait_recv()
            return unused

        lax.fori_loop(0, n - 1, one, 0)

    wait_recv(0, kbuf)
    wait_recv(1, vbuf)
    loads[3].wait()
    loads[4].wait()

    factor = math.log2(math.e) / math.sqrt(HD)
    span = CHUNK * rows
    text_valid = lax.broadcasted_iota(jnp.int32, (span, text), 1) < text_len[0]

    def attend(first_slot):
        q = qbuf[pl.ds(pl.multiple_of(first_slot * rows, rows), span), :]
        across = (((1,), (1,)), ((), ()))
        image = lax.dot_general(
            q, kbuf[pl.ds(0, n * rows), :], across, preferred_element_type=jnp.float32
        )
        words = lax.dot_general(
            q, kbuf[pl.ds(n * rows, text), :], across, preferred_element_type=jnp.float32
        )
        words = jnp.where(text_valid, words, -jnp.inf)
        peak = jnp.maximum(
            jnp.max(image, axis=1, keepdims=True), jnp.max(words, axis=1, keepdims=True)
        )
        image = jnp.exp2((image - peak) * factor)
        words = jnp.exp2((words - peak) * factor)
        total = jnp.sum(image, axis=1, keepdims=True) + jnp.sum(words, axis=1, keepdims=True)
        mixed = jnp.dot(
            image.astype(jnp.bfloat16),
            vbuf[pl.ds(0, n * rows), :],
            preferred_element_type=jnp.float32,
        ) + jnp.dot(
            words.astype(jnp.bfloat16),
            vbuf[pl.ds(n * rows, text), :],
            preferred_element_type=jnp.float32,
        )
        return (mixed / total).astype(jnp.bfloat16)

    def returning(j):
        u, b = behind(j)
        return pltpu.make_async_remote_copy(
            src_ref=obuf.at[slot(j)],
            dst_ref=att.at[j],
            send_sem=osend_sem.at[j],
            recv_sem=orecv_sem.at[j],
            device_id={"uly": u, "blk": b},
            device_id_type=pl.DeviceIdType.MESH,
        )

    def chunk(c, unused):
        first_slot = n - CHUNK - c * CHUNK
        for k in range(CHUNK):
            outgoing(2, qbuf, first_slot + k).wait_recv()
        obuf[pl.ds(pl.multiple_of(first_slot * rows, rows), span), :] = attend(first_slot)
        for k in range(CHUNK):
            returning(first_slot + k).start()
        return unused

    lax.fori_loop(0, n // CHUNK - 1, chunk, 0)
    for k in range(1, CHUNK):
        outgoing(2, qbuf, k).wait_recv()
    mixed = attend(0)
    obuf[pl.ds(0, span), :] = mixed
    for k in range(1, CHUNK):
        returning(k).start()
    att[0] = mixed[:rows]

    hidden = jnp.zeros((rows, gate.shape[1]), jnp.float32)
    group = 4
    for g in range(n // group - 1, -1, -1):
        for j in range(g * group, (g + 1) * group):
            weight_load(j).wait()
            if j > 0:
                returning(j).wait_recv()
        here = jnp.concatenate([att[j] for j in range(g * group, (g + 1) * group)], axis=1)
        hidden = hidden + jnp.dot(
            here,
            weight[pl.ds(g * group * HD, group * HD), :],
            preferred_element_type=jnp.float32,
        )
    loads[5].wait()
    loads[6].wait()
    hidden = res[...].astype(jnp.float32) + gate[...] * (hidden + mlp[...].astype(jnp.float32))
    center = jnp.mean(hidden, axis=1, keepdims=True)
    hidden = hidden - center
    variance = jnp.mean(hidden * hidden, axis=1, keepdims=True)
    hidden = hidden * (1.0 / jnp.sqrt(variance + 1e-06))
    modulated = (hidden * (1.0 + scale[...]) + shift[...]).astype(jnp.bfloat16)
    loads[7].wait()
    cond = lax.dot_general(
        fw[...], modulated, (((1,), (1,)), ((), ())), preferred_element_type=jnp.float32
    ) + jnp.transpose(jnp.broadcast_to(bias[...], (rows, bias.shape[1])))
    strength = jnp.full((1, 1), guidance[0], jnp.int32).astype(jnp.float32) / 10.0
    velocity = uncond[...] + strength * (cond - uncond[...])
    index = jnp.full((1, 1), timestep[0], jnp.int32).astype(jnp.float32)
    delta = sigma_of(1.0 - (index + 1.0) / STEPS) - sigma_of(1.0 - index / STEPS)
    vel_out[...] = velocity
    next_out[...] = latents[...] + delta * velocity

    def drain(j, unused):
        outgoing(0, kbuf, j).wait_send()
        outgoing(1, vbuf, j).wait_send()
        outgoing(2, qbuf, j).wait_send()
        returning(j).wait_send()
        return unused

    lax.fori_loop(1, n, drain, 0)


def fused_body(
    queries,
    keys,
    values,
    text_keys,
    text_values,
    text_len,
    residual,
    mlp_term,
    gate,
    final_shift,
    final_scale,
    final_weight,
    final_bias,
    out_weight,
    uncond_velocity,
    latents,
    timestep,
    guidance,
):
    uly_size = lax.axis_size("uly")
    blk_size = lax.axis_size("blk")
    n = uly_size * blk_size
    rows = queries.shape[0]
    text = text_keys.shape[0]
    width = residual.shape[1]
    anywhere = pl.BlockSpec(memory_space=pl.ANY)
    vmem = pl.BlockSpec(memory_space=pltpu.VMEM)
    smem = pl.BlockSpec(memory_space=pltpu.SMEM)
    result = jax.ShapeDtypeStruct(latents.shape[::-1], jnp.float32)
    bf16 = jnp.bfloat16
    velocity, next_latents = pl.pallas_call(
        functools.partial(fused_kernel, uly_size, blk_size),
        out_shape=(result, result),
        in_specs=[anywhere] * 5
        + [smem]
        + [anywhere] * 2
        + [vmem] * 3
        + [anywhere, vmem, anywhere, vmem, vmem, smem, smem],
        out_specs=(vmem, vmem),
        scratch_shapes=[
            pltpu.VMEM((3, rows, HEADS * HD), bf16),
            pltpu.VMEM((3, n * rows, HD), bf16),
            pltpu.VMEM((n * rows, HD), bf16),
            pltpu.VMEM((n * rows + text, HD), bf16),
            pltpu.VMEM((n * rows + text, HD), bf16),
            pltpu.VMEM((n * rows, HD), bf16),
            pltpu.VMEM((n, rows, HD), bf16),
            pltpu.VMEM((HEADS * HD, width), bf16),
            pltpu.VMEM((rows, width), bf16),
            pltpu.VMEM((rows, width), bf16),
            pltpu.VMEM(final_weight.shape[::-1], bf16),
            pltpu.SemaphoreType.DMA((8,)),
            pltpu.SemaphoreType.DMA((n,)),
            pltpu.SemaphoreType.DMA((3, n)),
            pltpu.SemaphoreType.DMA((3, n)),
            pltpu.SemaphoreType.DMA((n,)),
            pltpu.SemaphoreType.DMA((n,)),
        ],
        compiler_params=pltpu.CompilerParams(
            collective_id=0, has_side_effects=True, vmem_limit_bytes=56 * 2**20
        ),
    )(
        queries,
        keys,
        values,
        text_keys,
        text_values,
        text_len,
        residual,
        mlp_term,
        gate.reshape(1, width),
        final_shift.reshape(1, width),
        final_scale.reshape(1, width),
        final_weight.T,
        final_bias.reshape(1, -1),
        out_weight,
        uncond_velocity.T,
        latents.T,
        timestep,
        guidance,
    )
    return velocity.T, next_latents.T


def solution(mesh):
    placed = (
        P(("cfg", "uly", "blk"), None),
        P(("cfg", "uly", "blk"), None),
        P(("cfg", "uly", "blk"), None),
        P("cfg", None),
        P("cfg", None),
        P("cfg"),
        P(("cfg", "uly", "blk"), None),
        P(("cfg", "uly", "blk"), None),
        P(),
        P(),
        P(),
        P(),
        P(),
        P(),
        P(("cfg", "uly", "blk"), None),
        P(("cfg", "uly", "blk"), None),
        P(),
        P(),
    )
    return jax.shard_map(
        fused_body if mesh.shape["uly"] * mesh.shape["blk"] == HEADS else body,
        mesh=mesh,
        in_specs=placed,
        out_specs=(P(("cfg", "uly", "blk"), None), P(("cfg", "uly", "blk"), None)),
        check_vma=False,
    )
```

```python
import functools
import math

import jax
import jax.numpy as jnp
from jax import lax
from jax.experimental import pallas as pl
from jax.experimental.pallas import tpu as pltpu
from jax.sharding import PartitionSpec as P

HEADS = 16
HD = 128
STEPS = 50


def power_of_two(exponent):
    shifted = exponent + 64
    result = jnp.full(exponent.shape, 2.0 ** (-64), jnp.float32)
    for position in range(7):
        result = jnp.where(shifted // 2**position % 2 == 1, result * 2.0**2**position, result)
    return result


def floor_log2(magnitude, lowest, highest):
    octave = jnp.full(magnitude.shape, lowest, jnp.int32)
    for degree in range(lowest + 1, highest + 1):
        octave = octave + (magnitude >= 2.0**degree).astype(jnp.int32)
    return octave


def coarse_grid(scaled):
    magnitude = jnp.abs(scaled)
    octave = floor_log2(magnitude, -6, 8)
    ratio = magnitude * power_of_two(3 - octave)
    nearest = jnp.floor(ratio + 0.5)
    halfway = nearest - ratio == 0.5
    is_odd = nearest - 2.0 * jnp.floor(nearest * 0.5) == 1.0
    nearest = jnp.where(halfway & is_odd, nearest - 1.0, nearest)
    return jnp.sign(scaled) * jnp.minimum(nearest * power_of_two(octave - 3), 448.0)


def encode_blocks(entries):
    count, heads_here, width = entries.shape
    blocks = entries.astype(jnp.float32).reshape(count, heads_here, width // 32, 32)
    largest = jnp.max(jnp.abs(blocks), axis=3)
    exponent = floor_log2(largest, -20, 7) - 8
    payload = coarse_grid(blocks * power_of_two(-exponent)[:, :, :, None])
    return (payload.reshape(count, heads_here, width).astype(jnp.bfloat16), exponent)


def decode_blocks(payload, exponent):
    count, heads_here, width = payload.shape
    blocks = payload.astype(jnp.float32).reshape(count, heads_here, width // 32, 32)
    decoded = blocks * power_of_two(exponent)[:, :, :, None]
    return decoded.reshape(count, heads_here, width).astype(jnp.bfloat16)


def text_start(query_rows, text_key_heads, text_value_heads, text_len):
    scaling = 1.0 / math.sqrt(HD)
    scores = (
        jnp.einsum("shd,thd->sht", query_rows, text_key_heads, preferred_element_type=jnp.float32)
        * scaling
    )
    valid = jnp.arange(text_key_heads.shape[0]) < text_len[0]
    scores = jnp.where(valid[None, None, :], scores, -jnp.inf)
    peak = jnp.max(scores, axis=2)
    weights = jnp.exp(scores - peak[:, :, None])
    total = jnp.sum(weights, axis=2)
    summed = jnp.einsum(
        "sht,thd->shd",
        weights.astype(jnp.bfloat16),
        text_value_heads,
        preferred_element_type=jnp.float32,
    )
    return (peak, total, summed)


def attend_block(running, query_rows, block_keys, block_values):
    scaling = 1.0 / math.sqrt(HD)
    peak, total, summed = running
    scores = (
        jnp.einsum("shd,khd->shk", query_rows, block_keys, preferred_element_type=jnp.float32)
        * scaling
    )
    new_peak = jnp.maximum(peak, jnp.max(scores, axis=2))
    correction = jnp.exp(peak - new_peak)
    weights = jnp.exp(scores - new_peak[:, :, None])
    total = total * correction + jnp.sum(weights, axis=2)
    added = jnp.einsum(
        "shk,khd->shd",
        weights.astype(jnp.bfloat16),
        block_values,
        preferred_element_type=jnp.float32,
    )
    summed = summed * correction[:, :, None] + added
    return (new_peak, total, summed)


def key_fold(carried, portion, query_rows):
    key_part, value_part = portion
    count = key_part.shape[0]
    width = 512
    key_blocks = key_part.reshape((count // width, width) + key_part.shape[1:])
    value_blocks = value_part.reshape((count // width, width) + value_part.shape[1:])

    def one_block(running, blocks):
        return (attend_block(running, query_rows, blocks[0], blocks[1]), None)

    final_state, unused = lax.scan(one_block, carried, (key_blocks, value_blocks))
    return final_state


def finish_rows(carried):
    peak, total, summed = carried
    return (summed / total[:, :, None]).astype(jnp.bfloat16)


def sigma_of(moment):
    return 7.0 * moment / (1.0 + 6.0 * moment)


def body(
    queries,
    keys,
    values,
    text_keys,
    text_values,
    text_len,
    residual,
    mlp_term,
    gate,
    final_shift,
    final_scale,
    final_weight,
    final_bias,
    out_weight,
    uncond_velocity,
    latents,
    timestep,
    guidance,
):
    rows_here = queries.shape[0]
    query_three = queries.reshape(rows_here, HEADS, HD)
    key_three = keys.reshape(rows_here, HEADS, HD)
    value_three = values.reshape(rows_here, HEADS, HD)
    text_key_three = text_keys.reshape(text_keys.shape[0], HEADS, HD)
    text_value_three = text_values.reshape(text_values.shape[0], HEADS, HD)
    query_pay, query_exp = encode_blocks(query_three)
    key_pay, key_exp = encode_blocks(key_three)
    value_pay, value_exp = encode_blocks(value_three)
    local_heads = HEADS // lax.axis_size("uly")
    first_head = lax.axis_index("uly") * local_heads
    query_pay, query_exp, key_pay, key_exp, value_pay, value_exp = (
        lax.all_to_all(query_pay, "uly", split_axis=1, concat_axis=0, tiled=True),
        lax.all_to_all(query_exp, "uly", split_axis=1, concat_axis=0, tiled=True),
        lax.all_to_all(key_pay, "uly", split_axis=1, concat_axis=0, tiled=True),
        lax.all_to_all(key_exp, "uly", split_axis=1, concat_axis=0, tiled=True),
        lax.all_to_all(value_pay, "uly", split_axis=1, concat_axis=0, tiled=True),
        lax.all_to_all(value_exp, "uly", split_axis=1, concat_axis=0, tiled=True),
    )
    query_rows = decode_blocks(query_pay, query_exp)
    key_rows = decode_blocks(key_pay, key_exp)
    value_rows = decode_blocks(value_pay, value_exp)
    text_key_heads = lax.dynamic_slice_in_dim(text_key_three, first_head, local_heads, 1)
    text_value_heads = lax.dynamic_slice_in_dim(text_value_three, first_head, local_heads, 1)
    initial = text_start(query_rows, text_key_heads, text_value_heads, text_len)
    carried = key_fold(
        initial,
        (
            lax.all_gather(key_rows, "blk", axis=0, tiled=True),
            lax.all_gather(value_rows, "blk", axis=0, tiled=True),
        ),
        query_rows,
    )
    attention_rows = lax.all_to_all(
        finish_rows(carried), "uly", split_axis=0, concat_axis=1, tiled=True
    )
    attention = attention_rows.reshape(rows_here, HEADS * HD)
    projected = jnp.dot(attention, out_weight, preferred_element_type=jnp.float32)
    hidden = residual.astype(jnp.float32) + gate[None, :] * (
        projected + mlp_term.astype(jnp.float32)
    )
    center = jnp.mean(hidden, axis=1, keepdims=True)
    spread = jnp.mean((hidden - center) ** 2, axis=1, keepdims=True)
    normed = (hidden - center) / jnp.sqrt(spread + 1e-06)
    modulated = (normed * (1.0 + final_scale[None, :]) + final_shift[None, :]).astype(jnp.bfloat16)
    cond_velocity = (
        jnp.dot(modulated, final_weight, preferred_element_type=jnp.float32) + final_bias[None, :]
    )
    factor = guidance[0].astype(jnp.float32) / 10.0
    velocity = uncond_velocity + factor * (cond_velocity - uncond_velocity)
    index = timestep[0].astype(jnp.float32)
    delta = sigma_of(1.0 - (index + 1.0) / STEPS) - sigma_of(1.0 - index / STEPS)
    next_latents = latents + delta * velocity
    return (velocity, next_latents)


CHUNK = 4
SUB = 2


def block_round(entries, spread_matrix):
    x = entries.astype(jnp.float32)
    size = jnp.abs(x)
    top = size
    for shift in (1, 2, 4, 8, 16):
        top = jnp.maximum(top, pltpu.roll(top, shift, 1))
    top = jnp.maximum(top, 2.0**-20)
    top = top * 0.7515
    carrier = top * 2.0**23
    top = (top + carrier) - carrier
    scale = jnp.dot(
        top.astype(jnp.bfloat16), spread_matrix, preferred_element_type=jnp.float32
    )
    carrier = jnp.maximum(size * 2.0**20, scale * 96.0)
    rounded = (x + carrier) - carrier
    limit = scale * 1.75
    return jnp.minimum(jnp.maximum(rounded, -limit), limit).astype(jnp.bfloat16)


def fused_kernel(
    uly_size,
    blk_size,
    q_hbm,
    k_hbm,
    v_hbm,
    tk_hbm,
    tv_hbm,
    text_len,
    res_hbm,
    mlp_hbm,
    gate,
    shift,
    scale,
    fw_hbm,
    bias,
    ow_hbm,
    cond_out,
    raw,
    coded,
    qbuf,
    kbuf,
    vbuf,
    vwide,
    obuf,
    att,
    weight,
    res,
    mlp,
    fw,
    load_sem,
    weight_sem,
    send_sem,
    recv_sem,
    osend_sem,
    orecv_sem,
):
    n = uly_size * blk_size
    rows = raw.shape[1]
    uly = lax.axis_index("uly")
    blk = lax.axis_index("blk")
    me = uly * blk_size + blk

    def ahead(j):
        return lax.rem(uly + lax.rem(j, uly_size), uly_size), lax.rem(
            blk + j // uly_size, blk_size
        )

    def behind(j):
        return lax.rem(uly + uly_size - lax.rem(j, uly_size), uly_size), lax.rem(
            blk + blk_size - j // uly_size, blk_size
        )

    barrier = pltpu.get_barrier_semaphore()

    def greet(j, unused):
        u, b = ahead(j)
        pl.semaphore_signal(
            barrier, inc=1, device_id={"uly": u, "blk": b}, device_id_type=pl.DeviceIdType.MESH
        )
        return unused

    own = pl.ds(pl.multiple_of(me * HD, HD), HD)
    text = tk_hbm.shape[0]
    loads = [
        pltpu.make_async_copy(k_hbm, raw.at[0], load_sem.at[0]),
        pltpu.make_async_copy(v_hbm, raw.at[1], load_sem.at[1]),
        pltpu.make_async_copy(q_hbm, raw.at[2], load_sem.at[2]),
        pltpu.make_async_copy(tk_hbm.at[:, own], kbuf.at[pl.ds(n * rows, text)], load_sem.at[3]),
        pltpu.make_async_copy(tv_hbm.at[:, own], vbuf.at[pl.ds(n * rows, text)], load_sem.at[4]),
        pltpu.make_async_copy(res_hbm, res, load_sem.at[5]),
        pltpu.make_async_copy(mlp_hbm, mlp, load_sem.at[6]),
        pltpu.make_async_copy(fw_hbm, fw, load_sem.at[7]),
    ]
    for load in loads:
        load.start()
    lax.fori_loop(1, n, greet, 0)

    lane_from = lax.broadcasted_iota(jnp.int32, (HD, HD), 0)
    lane_to = lax.broadcasted_iota(jnp.int32, (HD, HD), 1)
    spread_matrix = jnp.where(lane_from == lane_to // 32 * 32 + 31, 1.0, 0.0).astype(jnp.bfloat16)

    def slot(j):
        return pl.ds(pl.multiple_of(j * rows, rows), rows)

    def outgoing(kind, target, j):
        u, b = ahead(j)
        return pltpu.make_async_remote_copy(
            src_ref=coded.at[kind, slot(j)],
            dst_ref=target.at[slot(j)],
            send_sem=send_sem.at[kind, j],
            recv_sem=recv_sem.at[kind, j],
            device_id={"uly": u, "blk": b},
            device_id_type=pl.DeviceIdType.MESH,
        )

    def weight_load(j):
        u, b = ahead(j)
        start = pl.multiple_of((u * blk_size + b) * HD, HD)
        return pltpu.make_async_copy(
            ow_hbm.at[pl.ds(start, HD)], weight.at[slot(j) if rows == HD else pl.ds(j * HD, HD)],
            weight_sem.at[j],
        )

    for kind, target in ((0, kbuf), (1, vbuf), (2, qbuf)):
        loads[kind].wait()

        def code(j):
            u, b = ahead(j)
            columns = pl.ds(pl.multiple_of((u * blk_size + b) * HD, HD), HD)
            return block_round(raw[kind, :, columns], spread_matrix)

        near = uly_size if kind == 2 else 1

        def code_and_send_near(j, unused):
            coded[kind, slot(j), :] = code(j)
            outgoing(kind, target, j).start()
            return unused

        if kind == 2:
            target[pl.ds(0, rows), :] = code(0)
            lax.fori_loop(1, near, code_and_send_near, 0)
        if kind == 0:

            def code_only(i, unused):
                j = n - 1 - i
                coded[kind, slot(j), :] = code(j)
                return unused

            lax.fori_loop(0, 2, code_only, 0)
            pl.semaphore_wait(barrier, n - 1)
            outgoing(kind, target, n - 1).start()
            outgoing(kind, target, n - 2).start()
            first = 2
        else:
            first = 0

        def code_and_send(i, unused):
            j = n - 1 - i
            coded[kind, slot(j), :] = code(j)
            outgoing(kind, target, j).start()
            return unused

        lax.fori_loop(first, n - near, code_and_send, 0)
        if kind != 2:
            target[pl.ds(0, rows), :] = code(0)

    def start_weight(i, unused):
        weight_load(n - 1 - i).start()
        return unused

    lax.fori_loop(0, n, start_weight, 0)

    def wait_recv(kind, target):
        def one(i, unused):
            outgoing(kind, target, n - 1 - i).wait_recv()
            return unused

        lax.fori_loop(0, n - 1, one, 0)

    vwide[:, HD:] = jnp.ones((vwide.shape[0], HD), jnp.bfloat16)
    wait_recv(0, kbuf)
    wait_recv(1, vbuf)
    loads[3].wait()
    loads[4].wait()
    vwide[:, :HD] = vbuf[...]

    factor = math.log2(math.e) / math.sqrt(HD)
    span = SUB * rows
    text_valid = lax.broadcasted_iota(jnp.int32, (span, text), 1) < text_len[0]

    def attend(first_slot):
        start = first_slot * rows
        if not isinstance(start, int):
            start = pl.multiple_of(start, span)
        q = qbuf[pl.ds(start, span), :]
        across = (((1,), (1,)), ((), ()))
        image = lax.dot_general(
            q, kbuf[pl.ds(0, n * rows), :], across, preferred_element_type=jnp.float32
        )
        words = lax.dot_general(
            q, kbuf[pl.ds(n * rows, text), :], across, preferred_element_type=jnp.float32
        )
        words = jnp.where(text_valid, words, -jnp.inf)
        peak = jnp.maximum(
            jnp.max(image, axis=1, keepdims=True), jnp.max(words, axis=1, keepdims=True)
        )
        image = jnp.exp2((image - peak) * factor)
        words = jnp.exp2((words - peak) * factor)
        mixed = jnp.dot(
            image.astype(jnp.bfloat16),
            vwide[pl.ds(0, n * rows), :],
            preferred_element_type=jnp.float32,
        ) + jnp.dot(
            words.astype(jnp.bfloat16),
            vwide[pl.ds(n * rows, text), :],
            preferred_element_type=jnp.float32,
        )
        return (mixed[:, :HD] / mixed[:, HD:]).astype(jnp.bfloat16)

    def returning(j):
        u, b = behind(j)
        return pltpu.make_async_remote_copy(
            src_ref=obuf.at[slot(j)],
            dst_ref=att.at[j],
            send_sem=osend_sem.at[j],
            recv_sem=orecv_sem.at[j],
            device_id={"uly": u, "blk": b},
            device_id_type=pl.DeviceIdType.MESH,
        )

    def attend_chunk(first_slot):
        for k in range(0, CHUNK, SUB):
            start = (first_slot + k) * rows
            if not isinstance(start, int):
                start = pl.multiple_of(start, span)
            obuf[pl.ds(start, span), :] = attend(first_slot + k)

    def chunk(c, unused):
        first_slot = n - CHUNK - c * CHUNK
        for k in range(CHUNK):
            outgoing(2, qbuf, first_slot + k).wait_recv()
        attend_chunk(first_slot)
        for k in range(CHUNK):
            returning(first_slot + k).start()
        return unused

    for first_slot in range(0, uly_size, CHUNK):
        for k in range(first_slot, first_slot + CHUNK):
            if k > 0:
                outgoing(2, qbuf, k).wait_recv()
        attend_chunk(first_slot)
        for k in range(first_slot, first_slot + CHUNK):
            if k > 0:
                returning(k).start()
    lax.fori_loop(0, (n - uly_size) // CHUNK, chunk, 0)
    att[0] = obuf[pl.ds(0, rows), :]

    hidden = jnp.zeros((rows, gate.shape[1]), jnp.float32)
    group = uly_size
    for g in [0] + list(range(n // group - 1, 0, -1)):
        for j in range(g * group, (g + 1) * group):
            weight_load(j).wait()
            if j > 0:
                returning(j).wait_recv()
        here = jnp.concatenate([att[j] for j in range(g * group, (g + 1) * group)], axis=1)
        hidden = hidden + jnp.dot(
            here,
            weight[pl.ds(g * group * HD, group * HD), :],
            preferred_element_type=jnp.float32,
        )
    loads[5].wait()
    loads[6].wait()
    hidden = res[...].astype(jnp.float32) + gate[...] * (hidden + mlp[...].astype(jnp.float32))
    center = jnp.mean(hidden, axis=1, keepdims=True)
    hidden = hidden - center
    variance = jnp.mean(hidden * hidden, axis=1, keepdims=True)
    hidden = hidden * (1.0 / jnp.sqrt(variance + 1e-06))
    modulated = (hidden * (1.0 + scale[...]) + shift[...]).astype(jnp.bfloat16)
    loads[7].wait()
    cond = lax.dot_general(
        fw[...], modulated, (((1,), (1,)), ((), ())), preferred_element_type=jnp.float32
    ) + jnp.transpose(jnp.broadcast_to(bias[...], (rows, bias.shape[1])))
    cond_out[...] = cond

    def drain(j, unused):
        outgoing(0, kbuf, j).wait_send()
        outgoing(1, vbuf, j).wait_send()
        outgoing(2, qbuf, j).wait_send()
        returning(j).wait_send()
        return unused

    lax.fori_loop(1, n, drain, 0)


def fused_body(
    queries,
    keys,
    values,
    text_keys,
    text_values,
    text_len,
    residual,
    mlp_term,
    gate,
    final_shift,
    final_scale,
    final_weight,
    final_bias,
    out_weight,
    uncond_velocity,
    latents,
    timestep,
    guidance,
):
    uly_size = lax.axis_size("uly")
    blk_size = lax.axis_size("blk")
    n = uly_size * blk_size
    rows = queries.shape[0]
    text = text_keys.shape[0]
    width = residual.shape[1]
    anywhere = pl.BlockSpec(memory_space=pl.ANY)
    vmem = pl.BlockSpec(memory_space=pltpu.VMEM)
    smem = pl.BlockSpec(memory_space=pltpu.SMEM)
    result = jax.ShapeDtypeStruct(latents.shape[::-1], jnp.float32)
    bf16 = jnp.bfloat16
    cond_velocity = pl.pallas_call(
        functools.partial(fused_kernel, uly_size, blk_size),
        out_shape=result,
        in_specs=[anywhere] * 5
        + [smem]
        + [anywhere] * 2
        + [vmem] * 3
        + [anywhere, vmem, anywhere],
        out_specs=vmem,
        scratch_shapes=[
            pltpu.VMEM((3, rows, HEADS * HD), bf16),
            pltpu.VMEM((3, n * rows, HD), bf16),
            pltpu.VMEM((n * rows, HD), bf16),
            pltpu.VMEM((n * rows + text, HD), bf16),
            pltpu.VMEM((n * rows + text, HD), bf16),
            pltpu.VMEM((n * rows + text, 2 * HD), bf16),
            pltpu.VMEM((n * rows, HD), bf16),
            pltpu.VMEM((n, rows, HD), bf16),
            pltpu.VMEM((HEADS * HD, width), bf16),
            pltpu.VMEM((rows, width), bf16),
            pltpu.VMEM((rows, width), bf16),
            pltpu.VMEM(final_weight.shape[::-1], bf16),
            pltpu.SemaphoreType.DMA((8,)),
            pltpu.SemaphoreType.DMA((n,)),
            pltpu.SemaphoreType.DMA((3, n)),
            pltpu.SemaphoreType.DMA((3, n)),
            pltpu.SemaphoreType.DMA((n,)),
            pltpu.SemaphoreType.DMA((n,)),
        ],
        compiler_params=pltpu.CompilerParams(
            collective_id=0, has_side_effects=True, vmem_limit_bytes=56 * 2**20
        ),
    )(
        queries,
        keys,
        values,
        text_keys,
        text_values,
        text_len,
        residual,
        mlp_term,
        gate.reshape(1, width),
        final_shift.reshape(1, width),
        final_scale.reshape(1, width),
        final_weight.T,
        final_bias.reshape(1, -1),
        out_weight,
    )
    factor = guidance[0].astype(jnp.float32) / 10.0
    velocity = uncond_velocity + factor * (cond_velocity.T - uncond_velocity)
    index = timestep[0].astype(jnp.float32)
    delta = sigma_of(1.0 - (index + 1.0) / STEPS) - sigma_of(1.0 - index / STEPS)
    return velocity, latents + delta * velocity


def solution(mesh):
    placed = (
        P(("cfg", "uly", "blk"), None),
        P(("cfg", "uly", "blk"), None),
        P(("cfg", "uly", "blk"), None),
        P("cfg", None),
        P("cfg", None),
        P("cfg"),
        P(("cfg", "uly", "blk"), None),
        P(("cfg", "uly", "blk"), None),
        P(),
        P(),
        P(),
        P(),
        P(),
        P(),
        P(("cfg", "uly", "blk"), None),
        P(("cfg", "uly", "blk"), None),
        P(),
        P(),
    )
    return jax.shard_map(
        fused_body if mesh.shape["uly"] * mesh.shape["blk"] == HEADS else body,
        mesh=mesh,
        in_specs=placed,
        out_specs=(P(("cfg", "uly", "blk"), None), P(("cfg", "uly", "blk"), None)),
        check_vma=False,
    )
```

```python
import functools
import math

import jax
import jax.numpy as jnp
from jax import lax
from jax.experimental import pallas as pl
from jax.experimental.pallas import tpu as pltpu
from jax.sharding import PartitionSpec as P

HEADS = 16
HD = 128
STEPS = 50


def power_of_two(exponent):
    shifted = exponent + 64
    result = jnp.full(exponent.shape, 2.0 ** (-64), jnp.float32)
    for position in range(7):
        result = jnp.where(shifted // 2**position % 2 == 1, result * 2.0**2**position, result)
    return result


def floor_log2(magnitude, lowest, highest):
    octave = jnp.full(magnitude.shape, lowest, jnp.int32)
    for degree in range(lowest + 1, highest + 1):
        octave = octave + (magnitude >= 2.0**degree).astype(jnp.int32)
    return octave


def coarse_grid(scaled):
    magnitude = jnp.abs(scaled)
    octave = floor_log2(magnitude, -6, 8)
    ratio = magnitude * power_of_two(3 - octave)
    nearest = jnp.floor(ratio + 0.5)
    halfway = nearest - ratio == 0.5
    is_odd = nearest - 2.0 * jnp.floor(nearest * 0.5) == 1.0
    nearest = jnp.where(halfway & is_odd, nearest - 1.0, nearest)
    return jnp.sign(scaled) * jnp.minimum(nearest * power_of_two(octave - 3), 448.0)


def encode_blocks(entries):
    count, heads_here, width = entries.shape
    blocks = entries.astype(jnp.float32).reshape(count, heads_here, width // 32, 32)
    largest = jnp.max(jnp.abs(blocks), axis=3)
    exponent = floor_log2(largest, -20, 7) - 8
    payload = coarse_grid(blocks * power_of_two(-exponent)[:, :, :, None])
    return (payload.reshape(count, heads_here, width).astype(jnp.bfloat16), exponent)


def decode_blocks(payload, exponent):
    count, heads_here, width = payload.shape
    blocks = payload.astype(jnp.float32).reshape(count, heads_here, width // 32, 32)
    decoded = blocks * power_of_two(exponent)[:, :, :, None]
    return decoded.reshape(count, heads_here, width).astype(jnp.bfloat16)


def text_start(query_rows, text_key_heads, text_value_heads, text_len):
    scaling = 1.0 / math.sqrt(HD)
    scores = (
        jnp.einsum("shd,thd->sht", query_rows, text_key_heads, preferred_element_type=jnp.float32)
        * scaling
    )
    valid = jnp.arange(text_key_heads.shape[0]) < text_len[0]
    scores = jnp.where(valid[None, None, :], scores, -jnp.inf)
    peak = jnp.max(scores, axis=2)
    weights = jnp.exp(scores - peak[:, :, None])
    total = jnp.sum(weights, axis=2)
    summed = jnp.einsum(
        "sht,thd->shd",
        weights.astype(jnp.bfloat16),
        text_value_heads,
        preferred_element_type=jnp.float32,
    )
    return (peak, total, summed)


def attend_block(running, query_rows, block_keys, block_values):
    scaling = 1.0 / math.sqrt(HD)
    peak, total, summed = running
    scores = (
        jnp.einsum("shd,khd->shk", query_rows, block_keys, preferred_element_type=jnp.float32)
        * scaling
    )
    new_peak = jnp.maximum(peak, jnp.max(scores, axis=2))
    correction = jnp.exp(peak - new_peak)
    weights = jnp.exp(scores - new_peak[:, :, None])
    total = total * correction + jnp.sum(weights, axis=2)
    added = jnp.einsum(
        "shk,khd->shd",
        weights.astype(jnp.bfloat16),
        block_values,
        preferred_element_type=jnp.float32,
    )
    summed = summed * correction[:, :, None] + added
    return (new_peak, total, summed)


def key_fold(carried, portion, query_rows):
    key_part, value_part = portion
    count = key_part.shape[0]
    width = 512
    key_blocks = key_part.reshape((count // width, width) + key_part.shape[1:])
    value_blocks = value_part.reshape((count // width, width) + value_part.shape[1:])

    def one_block(running, blocks):
        return (attend_block(running, query_rows, blocks[0], blocks[1]), None)

    final_state, unused = lax.scan(one_block, carried, (key_blocks, value_blocks))
    return final_state


def finish_rows(carried):
    peak, total, summed = carried
    return (summed / total[:, :, None]).astype(jnp.bfloat16)


def sigma_of(moment):
    return 7.0 * moment / (1.0 + 6.0 * moment)


def body(
    queries,
    keys,
    values,
    text_keys,
    text_values,
    text_len,
    residual,
    mlp_term,
    gate,
    final_shift,
    final_scale,
    final_weight,
    final_bias,
    out_weight,
    uncond_velocity,
    latents,
    timestep,
    guidance,
):
    rows_here = queries.shape[0]
    query_three = queries.reshape(rows_here, HEADS, HD)
    key_three = keys.reshape(rows_here, HEADS, HD)
    value_three = values.reshape(rows_here, HEADS, HD)
    text_key_three = text_keys.reshape(text_keys.shape[0], HEADS, HD)
    text_value_three = text_values.reshape(text_values.shape[0], HEADS, HD)
    query_pay, query_exp = encode_blocks(query_three)
    key_pay, key_exp = encode_blocks(key_three)
    value_pay, value_exp = encode_blocks(value_three)
    local_heads = HEADS // lax.axis_size("uly")
    first_head = lax.axis_index("uly") * local_heads
    query_pay, query_exp, key_pay, key_exp, value_pay, value_exp = (
        lax.all_to_all(query_pay, "uly", split_axis=1, concat_axis=0, tiled=True),
        lax.all_to_all(query_exp, "uly", split_axis=1, concat_axis=0, tiled=True),
        lax.all_to_all(key_pay, "uly", split_axis=1, concat_axis=0, tiled=True),
        lax.all_to_all(key_exp, "uly", split_axis=1, concat_axis=0, tiled=True),
        lax.all_to_all(value_pay, "uly", split_axis=1, concat_axis=0, tiled=True),
        lax.all_to_all(value_exp, "uly", split_axis=1, concat_axis=0, tiled=True),
    )
    query_rows = decode_blocks(query_pay, query_exp)
    key_rows = decode_blocks(key_pay, key_exp)
    value_rows = decode_blocks(value_pay, value_exp)
    text_key_heads = lax.dynamic_slice_in_dim(text_key_three, first_head, local_heads, 1)
    text_value_heads = lax.dynamic_slice_in_dim(text_value_three, first_head, local_heads, 1)
    initial = text_start(query_rows, text_key_heads, text_value_heads, text_len)
    carried = key_fold(
        initial,
        (
            lax.all_gather(key_rows, "blk", axis=0, tiled=True),
            lax.all_gather(value_rows, "blk", axis=0, tiled=True),
        ),
        query_rows,
    )
    attention_rows = lax.all_to_all(
        finish_rows(carried), "uly", split_axis=0, concat_axis=1, tiled=True
    )
    attention = attention_rows.reshape(rows_here, HEADS * HD)
    projected = jnp.dot(attention, out_weight, preferred_element_type=jnp.float32)
    hidden = residual.astype(jnp.float32) + gate[None, :] * (
        projected + mlp_term.astype(jnp.float32)
    )
    center = jnp.mean(hidden, axis=1, keepdims=True)
    spread = jnp.mean((hidden - center) ** 2, axis=1, keepdims=True)
    normed = (hidden - center) / jnp.sqrt(spread + 1e-06)
    modulated = (normed * (1.0 + final_scale[None, :]) + final_shift[None, :]).astype(jnp.bfloat16)
    cond_velocity = (
        jnp.dot(modulated, final_weight, preferred_element_type=jnp.float32) + final_bias[None, :]
    )
    factor = guidance[0].astype(jnp.float32) / 10.0
    velocity = uncond_velocity + factor * (cond_velocity - uncond_velocity)
    index = timestep[0].astype(jnp.float32)
    delta = sigma_of(1.0 - (index + 1.0) / STEPS) - sigma_of(1.0 - index / STEPS)
    next_latents = latents + delta * velocity
    return (velocity, next_latents)


CHUNK = 4
SUB = 2


def block_round(entries, spread_matrix):
    x = entries.astype(jnp.float32)
    size = jnp.abs(x)
    top = size
    for shift in (1, 2, 4, 8, 16):
        top = jnp.maximum(top, pltpu.roll(top, shift, 1))
    top = jnp.maximum(top, 2.0**-20)
    top = top * 0.7515
    carrier = top * 2.0**23
    top = (top + carrier) - carrier
    scale = jnp.dot(
        top.astype(jnp.bfloat16), spread_matrix, preferred_element_type=jnp.float32
    )
    carrier = jnp.maximum(size * 2.0**20, scale * 96.0)
    rounded = (x + carrier) - carrier
    limit = scale * 1.75
    return jnp.minimum(jnp.maximum(rounded, -limit), limit).astype(jnp.bfloat16)


def fused_kernel(
    uly_size,
    blk_size,
    q_hbm,
    k_hbm,
    v_hbm,
    tk_hbm,
    tv_hbm,
    len_hbm,
    res_hbm,
    mlp_hbm,
    gate_hbm,
    shift_hbm,
    scale_hbm,
    fw_hbm,
    bias_hbm,
    ow_hbm,
    cond_out,
    raw,
    coded,
    qbuf,
    kbuf,
    vbuf,
    vwide,
    obuf,
    att,
    weight,
    res,
    mlp,
    fw,
    gate,
    shift,
    scale,
    bias,
    text_len,
    load_sem,
    weight_sem,
    send_sem,
    recv_sem,
    osend_sem,
    orecv_sem,
):
    n = uly_size * blk_size
    rows = raw.shape[1]
    uly = lax.axis_index("uly")
    blk = lax.axis_index("blk")
    me = uly * blk_size + blk

    def ahead(j):
        return lax.rem(uly + lax.rem(j, uly_size), uly_size), lax.rem(
            blk + j // uly_size, blk_size
        )

    def behind(j):
        return lax.rem(uly + uly_size - lax.rem(j, uly_size), uly_size), lax.rem(
            blk + blk_size - j // uly_size, blk_size
        )

    barrier = pltpu.get_barrier_semaphore()

    def greet(j, unused):
        u, b = ahead(j)
        pl.semaphore_signal(
            barrier, inc=1, device_id={"uly": u, "blk": b}, device_id_type=pl.DeviceIdType.MESH
        )
        return unused

    own = pl.ds(pl.multiple_of(me * HD, HD), HD)
    text = tk_hbm.shape[0]
    loads = [
        pltpu.make_async_copy(k_hbm, raw.at[0], load_sem.at[0]),
        pltpu.make_async_copy(v_hbm, raw.at[1], load_sem.at[1]),
        pltpu.make_async_copy(q_hbm, raw.at[2], load_sem.at[2]),
        pltpu.make_async_copy(tk_hbm.at[:, own], kbuf.at[pl.ds(n * rows, text)], load_sem.at[3]),
        pltpu.make_async_copy(tv_hbm.at[:, own], vbuf.at[pl.ds(n * rows, text)], load_sem.at[4]),
        pltpu.make_async_copy(res_hbm, res, load_sem.at[5]),
        pltpu.make_async_copy(mlp_hbm, mlp, load_sem.at[6]),
        pltpu.make_async_copy(fw_hbm, fw, load_sem.at[7]),
        pltpu.make_async_copy(gate_hbm, gate, load_sem.at[8]),
        pltpu.make_async_copy(shift_hbm, shift, load_sem.at[9]),
        pltpu.make_async_copy(scale_hbm, scale, load_sem.at[10]),
        pltpu.make_async_copy(bias_hbm, bias, load_sem.at[11]),
        pltpu.make_async_copy(len_hbm, text_len, load_sem.at[12]),
    ]
    for load in loads:
        load.start()
    lax.fori_loop(1, n, greet, 0)

    lane_from = lax.broadcasted_iota(jnp.int32, (HD, HD), 0)
    lane_to = lax.broadcasted_iota(jnp.int32, (HD, HD), 1)
    spread_matrix = jnp.where(lane_from == lane_to // 32 * 32 + 31, 1.0, 0.0).astype(jnp.bfloat16)

    def spread_slot(i):
        return (blk_size - 1 - i % blk_size) * uly_size + uly_size - 1 - i // blk_size

    def slot(j):
        return pl.ds(pl.multiple_of(j * rows, rows), rows)

    def outgoing(kind, target, j):
        u, b = ahead(j)
        return pltpu.make_async_remote_copy(
            src_ref=coded.at[kind, slot(j)],
            dst_ref=target.at[slot(j)],
            send_sem=send_sem.at[kind, j],
            recv_sem=recv_sem.at[kind, j],
            device_id={"uly": u, "blk": b},
            device_id_type=pl.DeviceIdType.MESH,
        )

    def weight_load(j):
        u, b = ahead(j)
        start = pl.multiple_of((u * blk_size + b) * HD, HD)
        return pltpu.make_async_copy(
            ow_hbm.at[pl.ds(start, HD)], weight.at[slot(j) if rows == HD else pl.ds(j * HD, HD)],
            weight_sem.at[j],
        )

    for kind, target in ((0, kbuf), (1, vbuf), (2, qbuf)):
        loads[kind].wait()

        def code(j):
            u, b = ahead(j)
            columns = pl.ds(pl.multiple_of((u * blk_size + b) * HD, HD), HD)
            return block_round(raw[kind, :, columns], spread_matrix)

        near = uly_size if kind == 2 else 1

        def code_and_send_near(j, unused):
            coded[kind, slot(j), :] = code(j)
            outgoing(kind, target, j).start()
            return unused

        if kind == 2:
            target[pl.ds(0, rows), :] = code(0)
            lax.fori_loop(1, near, code_and_send_near, 0)
        if kind == 0:

            def code_only(i, unused):
                j = spread_slot(i)
                coded[kind, slot(j), :] = code(j)
                return unused

            lax.fori_loop(0, 2, code_only, 0)
            pl.semaphore_wait(barrier, n - 1)
            outgoing(kind, target, spread_slot(0)).start()
            outgoing(kind, target, spread_slot(1)).start()
            first = 2
        else:
            first = 0

        def code_and_send(i, unused):
            j = n - 1 - i if kind == 2 else spread_slot(i)
            coded[kind, slot(j), :] = code(j)
            outgoing(kind, target, j).start()
            return unused

        lax.fori_loop(first, n - near, code_and_send, 0)
        if kind != 2:
            target[pl.ds(0, rows), :] = code(0)

    def start_weight(i, unused):
        weight_load(n - 1 - i).start()
        return unused

    lax.fori_loop(0, n, start_weight, 0)

    def wait_recv(kind, target):
        def one(i, unused):
            outgoing(kind, target, n - 1 - i).wait_recv()
            return unused

        lax.fori_loop(0, n - 1, one, 0)

    vwide[:, HD:] = jnp.ones((vwide.shape[0], HD), jnp.bfloat16)
    wait_recv(0, kbuf)
    wait_recv(1, vbuf)
    loads[3].wait()
    loads[4].wait()
    loads[12].wait()
    vwide[:, :HD] = vbuf[...]

    factor = math.log2(math.e) / math.sqrt(HD)
    span = SUB * rows
    text_valid = lax.broadcasted_iota(jnp.int32, (span, text), 1) < text_len[0]

    def attend(first_slot):
        start = first_slot * rows
        if not isinstance(start, int):
            start = pl.multiple_of(start, span)
        q = qbuf[pl.ds(start, span), :]
        across = (((1,), (1,)), ((), ()))
        image = lax.dot_general(
            q, kbuf[pl.ds(0, n * rows), :], across, preferred_element_type=jnp.float32
        )
        words = lax.dot_general(
            q, kbuf[pl.ds(n * rows, text), :], across, preferred_element_type=jnp.float32
        )
        words = jnp.where(text_valid, words, -jnp.inf)
        peak = jnp.maximum(
            jnp.max(image, axis=1, keepdims=True), jnp.max(words, axis=1, keepdims=True)
        )
        image = jnp.exp2((image - peak) * factor)
        words = jnp.exp2((words - peak) * factor)
        mixed = jnp.dot(
            image.astype(jnp.bfloat16),
            vwide[pl.ds(0, n * rows), :],
            preferred_element_type=jnp.float32,
        ) + jnp.dot(
            words.astype(jnp.bfloat16),
            vwide[pl.ds(n * rows, text), :],
            preferred_element_type=jnp.float32,
        )
        return (mixed[:, :HD] / mixed[:, HD:]).astype(jnp.bfloat16)

    def returning(j):
        u, b = behind(j)
        return pltpu.make_async_remote_copy(
            src_ref=obuf.at[slot(j)],
            dst_ref=att.at[j],
            send_sem=osend_sem.at[j],
            recv_sem=orecv_sem.at[j],
            device_id={"uly": u, "blk": b},
            device_id_type=pl.DeviceIdType.MESH,
        )

    def attend_chunk(first_slot):
        for k in range(0, CHUNK, SUB):
            start = (first_slot + k) * rows
            if not isinstance(start, int):
                start = pl.multiple_of(start, span)
            obuf[pl.ds(start, span), :] = attend(first_slot + k)

    def chunk(c, unused):
        first_slot = n - CHUNK - c * CHUNK
        for k in range(CHUNK):
            outgoing(2, qbuf, first_slot + k).wait_recv()
        attend_chunk(first_slot)
        for k in range(CHUNK):
            returning(first_slot + k).start()
        return unused

    for first_slot in range(0, uly_size, CHUNK):
        for k in range(first_slot, first_slot + CHUNK):
            if k > 0:
                outgoing(2, qbuf, k).wait_recv()
        attend_chunk(first_slot)
        for k in range(first_slot, first_slot + CHUNK):
            if k > 0:
                returning(k).start()
    lax.fori_loop(0, (n - uly_size) // CHUNK, chunk, 0)
    att[0] = obuf[pl.ds(0, rows), :]

    hidden = jnp.zeros((rows, gate.shape[1]), jnp.float32)
    group = uly_size
    for g in [0] + list(range(n // group - 1, 0, -1)):
        for j in range(g * group, (g + 1) * group):
            weight_load(j).wait()
            if j > 0:
                returning(j).wait_recv()
        here = jnp.concatenate([att[j] for j in range(g * group, (g + 1) * group)], axis=1)
        hidden = hidden + jnp.dot(
            here,
            weight[pl.ds(g * group * HD, group * HD), :],
            preferred_element_type=jnp.float32,
        )
    loads[5].wait()
    loads[6].wait()
    for place in range(8, 12):
        loads[place].wait()
    hidden = res[...].astype(jnp.float32) + gate[...] * (hidden + mlp[...].astype(jnp.float32))
    center = jnp.mean(hidden, axis=1, keepdims=True)
    hidden = hidden - center
    variance = jnp.mean(hidden * hidden, axis=1, keepdims=True)
    hidden = hidden * (1.0 / jnp.sqrt(variance + 1e-06))
    modulated = (hidden * (1.0 + scale[...]) + shift[...]).astype(jnp.bfloat16)
    loads[7].wait()
    cond = lax.dot_general(
        fw[...], modulated, (((1,), (1,)), ((), ())), preferred_element_type=jnp.float32
    ) + jnp.transpose(jnp.broadcast_to(bias[...], (rows, bias.shape[1])))
    cond_out[...] = cond

    def drain(j, unused):
        outgoing(0, kbuf, j).wait_send()
        outgoing(1, vbuf, j).wait_send()
        outgoing(2, qbuf, j).wait_send()
        returning(j).wait_send()
        return unused

    lax.fori_loop(1, n, drain, 0)


def fused_body(
    queries,
    keys,
    values,
    text_keys,
    text_values,
    text_len,
    residual,
    mlp_term,
    gate,
    final_shift,
    final_scale,
    final_weight,
    final_bias,
    out_weight,
    uncond_velocity,
    latents,
    timestep,
    guidance,
):
    uly_size = lax.axis_size("uly")
    blk_size = lax.axis_size("blk")
    n = uly_size * blk_size
    rows = queries.shape[0]
    text = text_keys.shape[0]
    width = residual.shape[1]
    anywhere = pl.BlockSpec(memory_space=pl.ANY)
    vmem = pl.BlockSpec(memory_space=pltpu.VMEM)
    result = jax.ShapeDtypeStruct(latents.shape[::-1], jnp.float32)
    bf16 = jnp.bfloat16
    cond_velocity = pl.pallas_call(
        functools.partial(fused_kernel, uly_size, blk_size),
        out_shape=result,
        in_specs=[anywhere] * 14,
        out_specs=vmem,
        scratch_shapes=[
            pltpu.VMEM((3, rows, HEADS * HD), bf16),
            pltpu.VMEM((3, n * rows, HD), bf16),
            pltpu.VMEM((n * rows, HD), bf16),
            pltpu.VMEM((n * rows + text, HD), bf16),
            pltpu.VMEM((n * rows + text, HD), bf16),
            pltpu.VMEM((n * rows + text, 2 * HD), bf16),
            pltpu.VMEM((n * rows, HD), bf16),
            pltpu.VMEM((n, rows, HD), bf16),
            pltpu.VMEM((HEADS * HD, width), bf16),
            pltpu.VMEM((rows, width), bf16),
            pltpu.VMEM((rows, width), bf16),
            pltpu.VMEM(final_weight.shape[::-1], bf16),
            pltpu.VMEM((1, width), jnp.float32),
            pltpu.VMEM((1, width), jnp.float32),
            pltpu.VMEM((1, width), jnp.float32),
            pltpu.VMEM((1, final_bias.shape[0]), jnp.float32),
            pltpu.SMEM((1,), jnp.int32),
            pltpu.SemaphoreType.DMA((13,)),
            pltpu.SemaphoreType.DMA((n,)),
            pltpu.SemaphoreType.DMA((3, n)),
            pltpu.SemaphoreType.DMA((3, n)),
            pltpu.SemaphoreType.DMA((n,)),
            pltpu.SemaphoreType.DMA((n,)),
        ],
        compiler_params=pltpu.CompilerParams(
            collective_id=0, has_side_effects=True, vmem_limit_bytes=56 * 2**20
        ),
    )(
        queries,
        keys,
        values,
        text_keys,
        text_values,
        text_len,
        residual,
        mlp_term,
        gate.reshape(1, width),
        final_shift.reshape(1, width),
        final_scale.reshape(1, width),
        final_weight.T,
        final_bias.reshape(1, -1),
        out_weight,
    )
    factor = guidance[0].astype(jnp.float32) / 10.0
    velocity = uncond_velocity + factor * (cond_velocity.T - uncond_velocity)
    index = timestep[0].astype(jnp.float32)
    delta = sigma_of(1.0 - (index + 1.0) / STEPS) - sigma_of(1.0 - index / STEPS)
    return velocity, latents + delta * velocity


def solution(mesh):
    placed = (
        P(("cfg", "uly", "blk"), None),
        P(("cfg", "uly", "blk"), None),
        P(("cfg", "uly", "blk"), None),
        P("cfg", None),
        P("cfg", None),
        P("cfg"),
        P(("cfg", "uly", "blk"), None),
        P(("cfg", "uly", "blk"), None),
        P(),
        P(),
        P(),
        P(),
        P(),
        P(),
        P(("cfg", "uly", "blk"), None),
        P(("cfg", "uly", "blk"), None),
        P(),
        P(),
    )
    return jax.shard_map(
        fused_body if mesh.shape["uly"] * mesh.shape["blk"] == HEADS else body,
        mesh=mesh,
        in_specs=placed,
        out_specs=(P(("cfg", "uly", "blk"), None), P(("cfg", "uly", "blk"), None)),
        check_vma=False,
    )
```
